256 devices in a mesh: replica: 32 (over x, z), shard: 8 (over y, core).
Axes of the slice: x: 4, y: 4, z: 8, core: 2. Of those that a mesh axis runs over, the one named last changes fastest.
Arguments:
- local_params: bfloat16 [32, 2048, 8192], P('replica', 'shard'), may hold values from -6 to 6
- shared_base: bfloat16 [2048, 8192], P('shard'), may hold values from -6 to 6
- momentum: float32 [2048, 8192], P('shard', 'replica'), may hold values from -6 to 6
Outputs:
- new_fragment: bfloat16 [2048, 8192], P('shard')
- new_momentum: float32 [2048, 8192], P('shard', 'replica')
The draws below stay inside these ranges and needn't reach their ends.
All inputs are finite; a program needn't handle non-finite values.
Results may differ from the reference program's by a relative error of at most 0.009.
Values may be sent and summed in bfloat16 or wider, within the bound.
No kernel may reach another device: no remote copies, remote signals or barrier semaphores. Data moves between devices by JAX's collectives and lax.ppermute only.
A program may use at most 128 MiB of HBM per device.

```python
import jax
import jax.numpy as jnp
from jax import lax

D = 8192
ROWS = 2048
REPLICAS = 32


def steps_of(rng, shape, shards, low, high):
    level = 1.0
    for dim, parts in shards:
        heights = jax.random.uniform(jax.random.fold_in(jax.random.fold_in(rng, 6), dim), (parts,), jnp.float32, low / len(shards), high / len(shards))
        level = level * jnp.repeat(jnp.exp(heights), shape[dim] // parts).reshape((-1,) + (1,) * (len(shape) - 1 - dim))
    return level


def noise(stream_key, extent, width, bound, cuts=(), kind=jnp.bfloat16):
    result = jax.random.normal(stream_key, extent, jnp.float32) * width
    if len(cuts) > 0:
        result = steps_of(stream_key, extent, cuts, -0.22, 0.18) * result
    return jnp.clip(result, min=-bound, max=bound).astype(kind)


def setup_inputs(seed: int = 0) -> dict:
    streams_of = jax.random.split(jax.random.key(seed), 4)
    local_params = noise(streams_of[0], (REPLICAS, ROWS, D), 1.0, 6.0, ((0, 32), (1, 8)))
    shared_base = noise(streams_of[1], (ROWS, D), 1.0, 6.0, ((0, 8),))
    momentum = noise(streams_of[2], (ROWS, D), 1.0, 6.0, ((0, 8), (1, 32)), jnp.float32)
    return {"local_params": local_params, "shared_base": shared_base, "momentum": momentum}


epsilon = 1e-06
outer_rate = 0.7
momentum_decay = 0.9
level_limit = 7.0
scale_factor = 2.0 / 7.0

def hadamard_pair():
    index = jnp.arange(64, dtype=jnp.int32)
    parity = jnp.zeros((64, 64), jnp.int32)
    for bit_number in range(6):
        parity = parity + (index[:, None] >> bit_number & index[None, :] >> bit_number & 1)
    signs = (1 - 2 * (parity % 2)).astype(jnp.float32)
    return jnp.kron(jnp.eye(2, dtype=jnp.float32), signs)

def rotate(values, table):
    flat = values.reshape(-1, 128)
    turned = jnp.dot(flat, table, precision=lax.Precision.HIGHEST, preferred_element_type=jnp.float32) / 8.0
    return turned.reshape(values.shape)

def compress(values):
    blocks = values.reshape(values.shape[0], -1, 64)
    scales = scale_factor * jnp.sqrt(lax.optimization_barrier(jnp.mean(blocks * blocks, axis=-1)) + epsilon)
    levels = jnp.clip(blocks / scales[..., None], -level_limit, level_limit).astype(jnp.bfloat16)
    return (levels.reshape(values.shape), scales)

def expand(levels, scales):
    blocks = levels.astype(jnp.float32).reshape(levels.shape[0], -1, 64)
    return (blocks * scales[..., None]).reshape(levels.shape)

def reference(local_params, shared_base, momentum):
    table = hadamard_pair()
    base_float = shared_base.astype(jnp.float32)

    def accumulate(summed, one_group):
        pseudo_grad = base_float - one_group.astype(jnp.float32)
        levels, scales = compress(rotate(pseudo_grad, table))
        return (summed + expand(levels, scales), None)
    summed, unused = lax.scan(accumulate, jnp.zeros(base_float.shape, jnp.float32), local_params)
    outer_grad = rotate(summed / float(REPLICAS), table)
    new_momentum = momentum_decay * momentum + outer_grad
    updated = base_float - outer_rate * (outer_grad + momentum_decay * new_momentum)
    new_fragment = updated.astype(jnp.bfloat16)
    return (new_fragment, new_momentum)
```

```python
import functools

import jax
import jax.numpy as jnp
import numpy as np
from jax import lax
from jax.experimental import pallas as pl
from jax.experimental.pallas import tpu as pltpu
from jax.sharding import PartitionSpec as P

epsilon = 1e-06
outer_rate = 0.7
momentum_decay = 0.9

NX, NZ = 4, 8
W = 256
ROWS_A = 144
ROWS_B = 112
BF, F32 = jnp.bfloat16, jnp.float32
VM = 48 * 2**20

Z_ORDER = (1, -2, 4, -1, 2, 0, 3, -3)
ANY = pl.BlockSpec(memory_space=pl.ANY)


def hadamard_blocks():
    index = np.arange(64)
    parity = np.zeros((64, 64), np.int64)
    for bit in range(6):
        parity += (index[:, None] >> bit) & (index[None, :] >> bit) & 1
    signs = (1 - 2 * (parity % 2)).astype(np.float32)
    return np.kron(np.eye(2, dtype=np.float32), signs) / 8.0


def params(**kw):
    return pltpu.CompilerParams(vmem_limit_bytes=VM, **kw)


def cost(flops, nbytes):
    return pl.CostEstimate(flops=flops, bytes_accessed=nbytes, transcendentals=0)


def position():
    replica = lax.axis_index("replica")
    return replica // NZ, lax.rem(replica, NZ)


def shift(value, dx, dz):
    pairs = [
        (x * NZ + z, (x + dx) % NX * NZ + (z + dz) % NZ) for x in range(NX) for z in range(NZ)
    ]
    return lax.ppermute(value, "replica", pairs)


def column_of(x, z, dx, dz):
    block = lax.rem(x + dx + NX, NX) * NZ + lax.rem(z + dz + NZ, NZ)
    return pl.multiple_of(block * W, W)


def contribute_kernel(row0, rows, slots, outs, place, local, base, turn, mean, *rest):
    out_refs = rest[: len(outs)]
    local_in, base_in, sent, in_sem, out_sem = rest[len(outs) :]
    x, z = place[0], place[1]

    def fetches(i, dx, dz):
        column = pl.ds(column_of(x, z, dx, dz), W)
        row = pl.ds(row0, rows)
        return (
            pltpu.make_async_copy(local.at[row, column], local_in.at[i], in_sem.at[0, i]),
            pltpu.make_async_copy(base.at[row, column], base_in.at[i], in_sem.at[1, i]),
        )

    for i, (dx, dz) in enumerate(slots):
        for copy in fetches(i, dx, dz):
            copy.start()
    first = 0
    for out, count in zip(out_refs, outs):

        def body(j, carry, out=out, first=first):
            i = first + j
            row = pl.ds(row0, rows)
            column = pl.ds(0, W)
            pltpu.make_async_copy(local.at[row, column], local_in.at[i], in_sem.at[0, i]).wait()
            pltpu.make_async_copy(base.at[row, column], base_in.at[i], in_sem.at[1, i]).wait()
            for half in range(2):
                lanes = pl.ds(half * 128, 128)
                pair = jnp.concatenate([base_in[i, :, lanes], local_in[i, :, lanes]], axis=1)
                rotated = jnp.dot(pair, turn[...], preferred_element_type=F32)
                square = rotated * rotated
                high = square.astype(BF)
                low = (square - high.astype(F32)).astype(BF)
                power = jnp.dot(
                    jnp.concatenate([high, low], axis=1), mean[...], preferred_element_type=F32
                )
                limit = 2.0 * jnp.sqrt(power + epsilon)
                sent[i, :, lanes] = jnp.clip(rotated, -limit, limit).astype(BF)
            target = out.at[:, pl.ds(pl.multiple_of(j * W, W), W)]
            pltpu.make_async_copy(sent.at[i], target, out_sem.at[i]).start()
            return carry

        lax.fori_loop(0, count, body, 0)
        first += count
    first = 0
    for out, count in zip(out_refs, outs):
        for j in range(count):
            target = out.at[:, pl.ds(j * W, W)]
            pltpu.make_async_copy(sent.at[first + j], target, out_sem.at[first + j]).wait()
        first += count


def contribute(row0, rows, slots, outs, place, local, base):
    table = hadamard_blocks()
    turn = jnp.asarray(np.concatenate([table, -table], axis=0), BF)
    ones = np.kron(np.eye(2, dtype=np.float32), np.ones((64, 64), np.float32)) / 64.0
    mean = jnp.asarray(np.concatenate([ones, ones], axis=0), BF)
    n = len(slots)
    return pl.pallas_call(
        functools.partial(contribute_kernel, row0, rows, slots, outs),
        out_shape=[jax.ShapeDtypeStruct((rows, count * W), BF) for count in outs],
        in_specs=[pl.BlockSpec(memory_space=pltpu.SMEM), ANY, ANY]
        + [pl.BlockSpec(memory_space=pltpu.VMEM)] * 2,
        out_specs=[ANY] * len(outs),
        scratch_shapes=[
            pltpu.VMEM((n, rows, W), BF),
            pltpu.VMEM((n, rows, W), BF),
            pltpu.VMEM((n, rows, W), BF),
            pltpu.SemaphoreType.DMA((2, n)),
            pltpu.SemaphoreType.DMA((n,)),
        ],
        compiler_params=params(),
        cost_estimate=cost(rows * 8192 * 1024, rows * 8192 * 6),
        name="contribute",
    )(place, local, base, turn, mean)


def call(kernel, outs, *args, nbytes=2**20, name=None):
    return pl.pallas_call(
        kernel,
        out_shape=[jax.ShapeDtypeStruct(s, d) for s, d in outs],
        in_specs=[pl.BlockSpec(memory_space=pltpu.VMEM)] * len(args),
        out_specs=[pl.BlockSpec(memory_space=pltpu.VMEM)] * len(outs),
        compiler_params=params(),
        cost_estimate=cost(nbytes, nbytes),
        name=name,
    )(*args)


def f(ref, start, size):
    return ref[:, pl.ds(start, size)].astype(F32)


def sum_x_kernel(a0, r1, r2, r3, plus, minus, keep0, keep3p, keep3m):
    for start, size, out in (
        (0, 640, plus),
        (640, 640, minus),
        (1280, 256, keep0),
        (1536, 256, keep3p),
        (1792, 256, keep3m),
    ):
        total = (f(a0, start, size) + f(r1, start, size)) + (f(r2, start, size) + f(r3, start, size))
        out[...] = total.astype(out.dtype)


def relay_kernel(w, keep3p, keep3m, from_minus, from_plus, to3p, to3m):
    h = w // 2
    to3p[:, pl.ds(0, h)] = (
        f(keep3p, 0, h) + f(from_plus, h + w, h) + f(from_minus, 2 * w, h)
    ).astype(BF)
    to3p[:, pl.ds(h, h)] = (f(keep3p, h, h) + f(from_plus, 2 * w, h)).astype(BF)
    to3m[:, pl.ds(0, h)] = (f(keep3m, 0, h) + f(from_minus, w, h)).astype(BF)
    to3m[:, pl.ds(h, h)] = (f(keep3m, h, h) + f(from_minus, w + h, h) + f(from_plus, 0, h)).astype(
        BF
    )


def near(w, keep0, from_minus, from_plus, r3p, r3m, start, size):
    return (f(keep0, start, size) + f(from_minus, start, size)) + (
        f(from_plus, w // 2 + start, size) + f(r3p, start, size) + f(r3m, start, size)
    )


def sum_z_kernel(keep0, from_minus, from_plus, r3p, r3m, own, s1, s2, s3):
    for k, out in enumerate((own, s1, s2, s3)):
        out[...] = near(NX * W, keep0, from_minus, from_plus, r3p, r3m, k * W, W).astype(out.dtype)


def update_kernel(
    place, keep0, from_minus, from_plus, r3p, r3m, own, b1, b2, b3, base, momentum, table,
    new_momentum, shard_a, shard_b, base_in, sem,
):
    columns = pl.ds(column_of(place[0], place[1], 0, 0), W)
    copy = pltpu.make_async_copy(base.at[:, columns], base_in, sem)
    copy.start()
    summed_a = near(W, keep0, from_minus, from_plus, r3p, r3m, 0, W)
    summed_b = (own[...] + b1[...].astype(F32)) + (b2[...].astype(F32) + b3[...].astype(F32))
    copy.wait()
    for row0, rows, summed, out in (
        (0, ROWS_A, summed_a, shard_a),
        (ROWS_A, ROWS_B, summed_b, shard_b),
    ):
        for half in range(2):
            lanes = pl.ds(half * 128, 128)
            row = pl.ds(row0, rows)
            outer_grad = jnp.dot(
                summed[:, half * 128 : half * 128 + 128] * (1.0 / 32.0),
                table[...],
                precision=lax.Precision.HIGHEST,
                preferred_element_type=F32,
            )
            moved = momentum_decay * momentum[row, lanes] + outer_grad
            new_momentum[row, lanes] = moved
            updated = base_in[row, lanes].astype(F32) - outer_rate * (
                outer_grad + momentum_decay * moved
            )
            out[:, lanes] = updated.astype(BF)


def update(place, base, momentum, *args):
    table = jnp.asarray(hadamard_blocks(), F32)
    vmem = pl.BlockSpec(memory_space=pltpu.VMEM)
    return pl.pallas_call(
        update_kernel,
        out_shape=[
            jax.ShapeDtypeStruct((ROWS_A + ROWS_B, W), F32),
            jax.ShapeDtypeStruct((ROWS_A, W), BF),
            jax.ShapeDtypeStruct((ROWS_B, W), BF),
        ],
        in_specs=[pl.BlockSpec(memory_space=pltpu.SMEM)] + [vmem] * 9 + [ANY] + [vmem] * 2,
        out_specs=[vmem] * 3,
        scratch_shapes=[pltpu.VMEM((ROWS_A + ROWS_B, W), BF), pltpu.SemaphoreType.DMA],
        compiler_params=params(),
        cost_estimate=cost(2**22, 2**20),
        name="update",
    )(place, *args, base, momentum, table)


def pieces_a():
    return (
        (0, 256, 0, 0), (256, 256, 3, 0), (512, 256, -3, 0), (768, 256, -1, 0), (1024, 256, 2, 0),
        (1280, 128, 4, 0), (1408, 256, 1, 0), (1664, 256, -2, 0), (1920, 128, 4, 128),
    )


def assemble_kernel(place, g0, g1, g2, g3, b0, b3p, b3m, bm, bp, out, sem):
    x, z = place[0], place[1]
    row_a, row_b = pl.ds(0, ROWS_A), pl.ds(ROWS_A, ROWS_B)
    copies = []

    def put(source, start, width, row, dx, dz, inner):
        block = lax.rem(x + dx + NX, NX) * NZ + lax.rem(z + dz + NZ, NZ)
        column = pl.ds(pl.multiple_of(block * W + inner, 128), width)
        k = len(copies)
        copy = pltpu.make_async_copy(source.at[:, pl.ds(start, width)], out.at[row, column], sem.at[k])
        copy.start()
        copies.append(copy)

    for e, block in enumerate((g0, g1, g2, g3)):
        for start, width, dz, inner in pieces_a():
            put(block, start, width, row_a, -e, dz, inner)
    for block, start, parts, dz, first in (
        (b0, 0, 4, 0, 0), (b3p, 0, 4, 3, 0), (b3m, 0, 4, -3, 0), (bm, 0, 4, -1, 0), (bm, 1024, 4, 2, 0),
        (bm, 2048, 2, 4, 0), (bp, 0, 4, 1, 0), (bp, 1024, 4, -2, 0), (bp, 2048, 2, 4, 2),
    ):
        for k in range(parts):
            put(block, start + k * W, W, row_b, -(first + k), dz, 0)
    for copy in copies:
        copy.wait()


def assemble(place, *blocks):
    return pl.pallas_call(
        assemble_kernel,
        out_shape=jax.ShapeDtypeStruct((ROWS_A + ROWS_B, NX * NZ * W), BF),
        in_specs=[pl.BlockSpec(memory_space=pltpu.SMEM)] + [ANY] * 9,
        out_specs=ANY,
        scratch_shapes=[pltpu.SemaphoreType.DMA((68,))],
        compiler_params=params(),
        cost_estimate=cost(0, 2**23),
        name="assemble",
    )(place, *blocks)


def shards(local_params, shared_base, momentum):
    x, z = position()
    place = jnp.stack([x, z]).astype(jnp.int32)
    local = local_params[0]
    slots_a = tuple((dx, dz) for dx in range(NX) for dz in Z_ORDER)
    slots_b = tuple((dx, dz) for dz in Z_ORDER for dx in range(NX))

    plus_b, minus_b, keep0_b, keep3p_b, keep3m_b = contribute(
        ROWS_A, ROWS_B, slots_b, (10, 10, 4, 4, 4), place, local, shared_base
    )
    a0, a1, a2, a3 = contribute(0, ROWS_A, slots_a, (8, 8, 8, 8), place, local, shared_base)
    from_minus_b, from_plus_b = shift(plus_b, 0, 1), shift(minus_b, 0, -1)
    r1, r2, r3 = shift(a1, 1, 0), shift(a2, 2, 0), shift(a3, 3, 0)

    half = (ROWS_B, NX * W)
    to3p, to3m = call(
        functools.partial(relay_kernel, NX * W), [(half, BF), (half, BF)],
        keep3p_b, keep3m_b, from_minus_b, from_plus_b, name="relay_b",
    )
    r3p, r3m = shift(to3p, 0, 3), shift(to3m, 0, -3)
    strip = (ROWS_B, W)
    own, s1, s2, s3 = call(
        sum_z_kernel, [(strip, F32), (strip, BF), (strip, BF), (strip, BF)],
        keep0_b, from_minus_b, from_plus_b, r3p, r3m, name="sum_b",
    )
    b1, b2, b3 = shift(s1, 1, 0), shift(s2, 2, 0), shift(s3, 3, 0)

    strip = (ROWS_A, W)
    group = (ROWS_A, 640)
    plus_a, minus_a, keep0, keep3p, keep3m = call(
        sum_x_kernel, [(group, BF), (group, BF), (strip, F32), (strip, F32), (strip, F32)],
        a0, r1, r2, r3, name="sum_a",
    )
    from_minus, from_plus = shift(plus_a, 0, 1), shift(minus_a, 0, -1)
    to3p, to3m = call(
        functools.partial(relay_kernel, W), [(strip, BF), (strip, BF)],
        keep3p, keep3m, from_minus, from_plus, name="relay_a",
    )
    r3p, r3m = shift(to3p, 0, 3), shift(to3m, 0, -3)

    new_momentum, own_a, own_b = update(
        place, shared_base, momentum, keep0, from_minus, from_plus, r3p, r3m, own, b1, b2, b3
    )

    p3, m3 = shift(own_a, 0, -3), shift(own_a, 0, 3)
    strips = [own_b] + [shift(own_b, e, 0) for e in (1, 2, 3)]
    from_minus = shift(jnp.concatenate([own_a, p3, m3[:, :128]], axis=1), 0, 1)
    from_plus = shift(jnp.concatenate([own_a, m3, p3[:, 128:]], axis=1), 0, -1)
    row_b = jnp.concatenate(strips, axis=1)
    p3_b, m3_b = shift(row_b, 0, -3), shift(row_b, 0, 3)
    from_minus_b = shift(jnp.concatenate([row_b, p3_b, m3_b[:, :512]], axis=1), 0, 1)
    from_plus_b = shift(jnp.concatenate([row_b, m3_b, p3_b[:, 512:]], axis=1), 0, -1)
    g0 = jnp.concatenate([own_a, p3, m3, from_minus, from_plus], axis=1)
    g1, g2, g3 = [shift(g0, e, 0) for e in (1, 2, 3)]
    new_fragment = assemble(
        place, g0, g1, g2, g3, row_b, p3_b, m3_b, from_minus_b, from_plus_b
    )
    return (new_fragment, new_momentum)


def solution(mesh):
    in_specs = (P("replica", "shard", None), P("shard", None), P("shard", "replica"))
    out_specs = (P("shard", None), P("shard", "replica"))
    return jax.shard_map(shards, mesh=mesh, in_specs=in_specs, out_specs=out_specs, check_vma=False)
```

```python
import functools

import jax
import jax.numpy as jnp
import numpy as np
from jax import lax
from jax.experimental import pallas as pl
from jax.experimental.pallas import tpu as pltpu
from jax.sharding import PartitionSpec as P

epsilon = 1e-06
outer_rate = 0.7
momentum_decay = 0.9

NX, NZ = 4, 8
W = 256
ROWS_A = 160
ROWS_B = 96
BF, F32 = jnp.bfloat16, jnp.float32
VM = 32 * 2**20
GROUP = 5

Z_ORDER = (1, -2, 4, -1, 2, 0, 3, -3)
ANY = pl.BlockSpec(memory_space=pl.ANY)


def hadamard_blocks():
    index = np.arange(64)
    parity = np.zeros((64, 64), np.int64)
    for bit in range(6):
        parity += (index[:, None] >> bit) & (index[None, :] >> bit) & 1
    signs = (1 - 2 * (parity % 2)).astype(np.float32)
    return np.kron(np.eye(2, dtype=np.float32), signs) / 8.0


def params(**kw):
    return pltpu.CompilerParams(vmem_limit_bytes=VM, **kw)


def cost(flops, nbytes):
    return pl.CostEstimate(flops=flops, bytes_accessed=nbytes, transcendentals=0)


def position():
    replica = lax.axis_index("replica")
    return replica // NZ, lax.rem(replica, NZ)


def shift(value, dx, dz):
    pairs = [
        (x * NZ + z, (x + dx) % NX * NZ + (z + dz) % NZ) for x in range(NX) for z in range(NZ)
    ]
    return lax.ppermute(value, "replica", pairs)


def column_of(x, z, dx, dz):
    block = lax.rem(x + dx + NX, NX) * NZ + lax.rem(z + dz + NZ, NZ)
    return pl.multiple_of(block * W, W)


def tables():
    row = lax.broadcasted_iota(jnp.int32, (256, 128), 0)
    column = lax.broadcasted_iota(jnp.int32, (256, 128), 1)
    bits = row & column & 63
    bits = bits ^ (bits >> 3)
    odd = (bits ^ (bits >> 1) ^ (bits >> 2)) & 1
    sign = (1 - 2 * odd).astype(F32) * 0.125
    sign = jnp.where(((row ^ column) & 64) == 0, sign, 0.0)
    turn = jnp.where(row < 128, sign, -sign).astype(BF)
    row = lax.broadcasted_iota(jnp.int32, (256, 256), 0)
    column = lax.broadcasted_iota(jnp.int32, (256, 256), 1)
    mean4 = jnp.where((row >> 6) == (column >> 6), 4.0 / 64.0, 0.0).astype(BF)
    return turn, mean4


def contribute_kernel(jobs, local, base, *rest):
    n_out = sum(len(outs) for _, _, _, outs in jobs)
    out_refs, rest = rest[:n_out], rest[n_out:]
    turn_ref, mean_ref, sem = rest[-3:]
    x, z = position()
    fetches = []
    k = 0
    for job, (row0, rows, slots, _) in enumerate(jobs):
        local_in, base_in = rest[2 * job : 2 * job + 2]
        for i, (dx, dz) in enumerate(slots):
            column = pl.ds(column_of(x, z, dx, dz), W)
            row = pl.ds(row0, rows)
            pair = (
                pltpu.make_async_copy(local.at[0, row, column], local_in.at[i], sem.at[0, k]),
                pltpu.make_async_copy(base.at[row, column], base_in.at[i], sem.at[1, k]),
            )
            for copy in pair:
                copy.start()
            fetches.append(pair)
            k += 1
    turn_ref[...], mean_ref[...] = tables()
    k = 0
    o = 0
    for job, (_, rows, _, outs) in enumerate(jobs):
        local_in, base_in = rest[2 * job : 2 * job + 2]
        first = 0
        for count in outs:
            for j0 in range(0, count, GROUP):
                group = min(GROUP, count - j0)
                i = first + j0
                for pair in fetches[k : k + group]:
                    for copy in pair:
                        copy.wait()
                k += group
                height = group * rows
                turned, squares = [], []
                for half in range(2):
                    lanes = pl.ds(half * 128, 128)
                    pair = jnp.concatenate(
                        [
                            base_in[i : i + group, :, lanes].reshape(height, 128),
                            local_in[i : i + group, :, lanes].reshape(height, 128),
                        ],
                        axis=1,
                    )
                    rotated = jnp.dot(pair, turn_ref[...], preferred_element_type=F32)
                    turned.append(rotated)
                    squares.append((rotated * rotated).astype(BF))
                power = jnp.dot(
                    jnp.concatenate(squares, axis=1), mean_ref[...], preferred_element_type=F32
                )
                power = power + 4.0 * epsilon
                limit = power * lax.rsqrt(power)
                for half in range(2):
                    bound = limit[:, half * 128 : half * 128 + 128]
                    value = jnp.minimum(jnp.maximum(turned[half], -bound), bound).astype(BF)
                    for g in range(group):
                        out_refs[o][:, pl.ds((j0 + g) * W + half * 128, 128)] = value[
                            g * rows : (g + 1) * rows
                        ]
            first += count
            o += 1


def contribute(jobs, local, base):
    n = sum(len(slots) for _, _, slots, _ in jobs)
    shapes = [
        jax.ShapeDtypeStruct((rows, count * W), BF) for _, rows, _, outs in jobs for count in outs
    ]
    scratch = []
    for _, rows, slots, _ in jobs:
        scratch += [pltpu.VMEM((len(slots), rows, W), BF)] * 2
    size = sum(rows * len(slots) * W for _, rows, slots, _ in jobs)
    return pl.pallas_call(
        functools.partial(contribute_kernel, jobs),
        out_shape=shapes,
        in_specs=[pl.BlockSpec(memory_space=pltpu.HBM)] * 2,
        out_specs=[pl.BlockSpec(memory_space=pltpu.VMEM)] * len(shapes),
        scratch_shapes=scratch
        + [
            pltpu.VMEM((256, 128), BF),
            pltpu.VMEM((256, 256), BF),
            pltpu.SemaphoreType.DMA((2, n)),
        ],
        compiler_params=params(),
        cost_estimate=cost(size * 1024, size * 6),
        name="contribute",
    )(local, base)


def call(kernel, outs, *args, nbytes=2**20, name=None):
    return pl.pallas_call(
        kernel,
        out_shape=[jax.ShapeDtypeStruct(s, d) for s, d in outs],
        in_specs=[pl.BlockSpec(memory_space=pltpu.VMEM)] * len(args),
        out_specs=[pl.BlockSpec(memory_space=pltpu.VMEM)] * len(outs),
        compiler_params=params(),
        cost_estimate=cost(nbytes, nbytes),
        name=name,
    )(*args)


def f(ref, start, size):
    return ref[:, pl.ds(start, size)].astype(F32)


def relay_x_kernel(near_pa, near_ma, near_mb, low, high, to_pa, to_ma, to_mb):
    to_pa[:, pl.ds(0, 1024)] = (f(near_pa, 0, 1024) + f(low, 0, 1024)).astype(BF)
    to_pa[:, pl.ds(1024, 256)] = near_pa[:, pl.ds(1024, 256)]
    to_ma[:, pl.ds(0, 1024)] = near_ma[:, pl.ds(0, 1024)]
    to_ma[:, pl.ds(1024, 256)] = (f(near_ma, 1024, 256) + f(high, 0, 256)).astype(BF)
    to_mb[...] = (f(near_mb, 0, 768) + f(high, 256, 768)).astype(BF)


def sum_x_kernel(own, r1, r2, *outs):
    start = 0
    for out in outs:
        size = out.shape[1]
        total = f(own, start, size) + f(r1, start, size) + f(r2, start, size)
        out[...] = total.astype(out.dtype)
        start += size


def relay_kernel(w, keep3p, keep3m, from_minus, from_plus, to3p, to3m):
    h = w // 2
    to3p[:, pl.ds(0, h)] = (
        f(keep3p, 0, h) + f(from_plus, h + w, h) + f(from_minus, 2 * w, h)
    ).astype(BF)
    to3p[:, pl.ds(h, h)] = (f(keep3p, h, h) + f(from_plus, 2 * w, h)).astype(BF)
    to3m[:, pl.ds(0, h)] = (f(keep3m, 0, h) + f(from_minus, w, h)).astype(BF)
    to3m[:, pl.ds(h, h)] = (f(keep3m, h, h) + f(from_minus, w + h, h) + f(from_plus, 0, h)).astype(
        BF
    )


def near(w, keep0, from_minus, from_plus, r3p, r3m, start, size):
    return (f(keep0, start, size) + f(from_minus, start, size)) + (
        f(from_plus, w // 2 + start, size) + f(r3p, start, size) + f(r3m, start, size)
    )


def sum_z_kernel(keep0, from_minus, from_plus, r3p, r3m, own, s1, s2, s3):
    for k, out in enumerate((own, s1, s2, s3)):
        out[...] = near(NX * W, keep0, from_minus, from_plus, r3p, r3m, k * W, W).astype(out.dtype)


def update_kernel(
    keep0, from_minus, from_plus, r3p, r3m, own, b1, b2, b3, base, momentum, table,
    new_momentum, shard_a, shard_b, base_in, sem,
):
    x, z = position()
    columns = pl.ds(column_of(x, z, 0, 0), W)
    copy = pltpu.make_async_copy(base.at[:, columns], base_in, sem)
    copy.start()
    summed_a = near(W, keep0, from_minus, from_plus, r3p, r3m, 0, W)
    summed_b = (own[...] + b1[...].astype(F32)) + (b2[...].astype(F32) + b3[...].astype(F32))
    copy.wait()
    for row0, rows, summed, out in (
        (0, ROWS_A, summed_a, shard_a),
        (ROWS_A, ROWS_B, summed_b, shard_b),
    ):
        for half in range(2):
            lanes = pl.ds(half * 128, 128)
            row = pl.ds(row0, rows)
            outer_grad = jnp.dot(
                summed[:, half * 128 : half * 128 + 128] * (1.0 / 32.0),
                table[...],
                precision=lax.Precision.HIGHEST,
                preferred_element_type=F32,
            )
            moved = momentum_decay * momentum[row, lanes] + outer_grad
            new_momentum[row, lanes] = moved
            updated = base_in[row, lanes].astype(F32) - outer_rate * (
                outer_grad + momentum_decay * moved
            )
            out[:, lanes] = updated.astype(BF)


def update(base, momentum, *args):
    table = jnp.asarray(hadamard_blocks(), F32)
    vmem = pl.BlockSpec(memory_space=pltpu.VMEM)
    return pl.pallas_call(
        update_kernel,
        out_shape=[
            jax.ShapeDtypeStruct((ROWS_A + ROWS_B, W), F32),
            jax.ShapeDtypeStruct((ROWS_A, W), BF),
            jax.ShapeDtypeStruct((ROWS_B, W), BF),
        ],
        in_specs=[vmem] * 9 + [pl.BlockSpec(memory_space=pltpu.HBM)] + [vmem] * 2,
        out_specs=[vmem] * 3,
        scratch_shapes=[pltpu.VMEM((ROWS_A + ROWS_B, W), BF), pltpu.SemaphoreType.DMA],
        compiler_params=params(),
        cost_estimate=cost(2**22, 2**20),
        name="update",
    )(*args, base, momentum, table)


PART_1 = ((0, 256, 0, 0), (256, 256, 3, 0), (512, 256, -3, 0))
PART_2 = (
    (0, 256, -1, 0), (256, 256, 2, 0), (512, 128, 4, 0),
    (640, 256, 1, 0), (896, 256, -2, 0), (1152, 128, 4, 128),
)
LOW = PART_1 + ((768, 256, -1, 0),)
HIGH = ((0, 256, 2, 0), (256, 128, 4, 0), (384, 256, 1, 0), (640, 256, -2, 0), (896, 128, 4, 128))


def assemble_kernel(o1, o2, m1, m2, p1, p2, low, high, b0, b3p, b3m, bm, bp, out, sem):
    x, z = position()
    row_a, row_b = pl.ds(0, ROWS_A), pl.ds(ROWS_A, ROWS_B)
    copies = []

    def put(source, start, width, row, dx, dz, inner):
        column = column_of(x, z, dx, dz) + inner
        column = pl.ds(pl.multiple_of(column, 128), width)
        k = len(copies)
        copy = pltpu.make_async_copy(source.at[:, pl.ds(start, width)], out.at[row, column], sem.at[k])
        copy.start()
        copies.append(copy)

    for source, dx, pieces in (
        (o1, 0, PART_1), (o2, 0, PART_2), (m1, -1, PART_1), (m2, -1, PART_2),
        (p1, 1, PART_1), (p2, 1, PART_2), (low, 2, LOW), (high, 2, HIGH),
    ):
        for start, width, dz, inner in pieces:
            put(source, start, width, row_a, dx, dz, inner)
    for block, start, parts, dz, first in (
        (b0, 0, 4, 0, 0), (b3p, 0, 4, 3, 0), (b3m, 0, 4, -3, 0), (bm, 0, 4, -1, 0), (bm, 1024, 4, 2, 0),
        (bm, 2048, 2, 4, 0), (bp, 0, 4, 1, 0), (bp, 1024, 4, -2, 0), (bp, 2048, 2, 4, 2),
    ):
        for k in range(parts):
            put(block, start + k * W, W, row_b, -(first + k), dz, 0)
    for copy in copies:
        copy.wait()


def assemble(*blocks):
    return pl.pallas_call(
        assemble_kernel,
        out_shape=jax.ShapeDtypeStruct((ROWS_A + ROWS_B, NX * NZ * W), BF),
        in_specs=[ANY] * len(blocks),
        out_specs=ANY,
        scratch_shapes=[pltpu.SemaphoreType.DMA((80,))],
        compiler_params=params(),
        cost_estimate=cost(0, 2**23),
        name="assemble",
    )(*blocks)


def shards(local, base, momentum):
    z_a, z_b = Z_ORDER[:5], Z_ORDER[5:]

    far = tuple((2, dz) for dz in Z_ORDER)
    far_low, far_high = contribute(((0, ROWS_A, far, (4, 4)),), local, base)
    sent_b = tuple((dx, dz) for dz in z_a for dx in range(NX))
    plus_b, minus_b = contribute(((ROWS_A, ROWS_B, sent_b, (10, 10)),), local, base)
    near = tuple((dx, dz) for dx in (1, -1, 0) for dz in Z_ORDER)
    kept_b = tuple((dx, dz) for dz in z_b for dx in range(NX))
    near_pa, near_pb, near_ma, near_mb, own_xa, own_xb, keep0_b, keep3p_b, keep3m_b = contribute(
        ((0, ROWS_A, near, (5, 3) * 3), (ROWS_A, ROWS_B, kept_b, (4, 4, 4))), local, base
    )
    low, high = shift(far_low, 1, 0), shift(far_high, -1, 0)
    from_minus_b, from_plus_b = shift(plus_b, 0, 1), shift(minus_b, 0, -1)

    wide, thin = (ROWS_A, 1280), (ROWS_A, 768)
    to_pa, to_ma, to_mb = call(
        relay_x_kernel, [(wide, BF), (wide, BF), (thin, BF)],
        near_pa, near_ma, near_mb, low, high, name="relay_x",
    )
    r_pa, r_ma = shift(to_pa, 1, 0), shift(to_ma, -1, 0)
    r_pb, r_mb = shift(near_pb, 1, 0), shift(to_mb, -1, 0)
    strip, group = (ROWS_A, W), (ROWS_A, 640)
    plus_a, minus_a = call(
        sum_x_kernel, [(group, BF), (group, BF)], own_xa, r_pa, r_ma, name="sum_a1"
    )
    from_minus, from_plus = shift(plus_a, 0, 1), shift(minus_a, 0, -1)
    keep0, keep3p, keep3m = call(
        sum_x_kernel, [(strip, F32)] * 3, own_xb, r_pb, r_mb, name="sum_a2"
    )

    half = (ROWS_B, NX * W)
    to3p, to3m = call(
        functools.partial(relay_kernel, NX * W), [(half, BF), (half, BF)],
        keep3p_b, keep3m_b, from_minus_b, from_plus_b, name="relay_b",
    )
    r3p_b, r3m_b = shift(to3p, 0, 3), shift(to3m, 0, -3)

    to3p, to3m = call(
        functools.partial(relay_kernel, W), [(strip, BF), (strip, BF)],
        keep3p, keep3m, from_minus, from_plus, name="relay_a",
    )
    r3p, r3m = shift(to3p, 0, 3), shift(to3m, 0, -3)

    strip = (ROWS_B, W)
    own, s1, s2, s3 = call(
        sum_z_kernel, [(strip, F32), (strip, BF), (strip, BF), (strip, BF)],
        keep0_b, from_minus_b, from_plus_b, r3p_b, r3m_b, name="sum_b",
    )
    b1, b2, b3 = shift(s1, 1, 0), shift(s2, 2, 0), shift(s3, 3, 0)

    new_momentum, own_a, own_b = update(
        base, momentum, keep0, from_minus, from_plus, r3p, r3m, own, b1, b2, b3
    )

    p3, m3 = shift(own_a, 0, -3), shift(own_a, 0, 3)
    strips = [own_b] + [shift(own_b, e, 0) for e in (1, 2, 3)]
    from_minus = shift(jnp.concatenate([own_a, p3, m3[:, :128]], axis=1), 0, 1)
    from_plus = shift(jnp.concatenate([own_a, m3, p3[:, 128:]], axis=1), 0, -1)
    part1 = jnp.concatenate([own_a, p3, m3], axis=1)
    m1, p1 = shift(part1, 1, 0), shift(part1, -1, 0)
    part2 = jnp.concatenate([from_minus, from_plus], axis=1)
    m2, p2 = shift(part2, 1, 0), shift(part2, -1, 0)
    low = shift(jnp.concatenate([m1, m2[:, :256]], axis=1), 1, 0)
    high = shift(p2[:, 256:], -1, 0)
    row_b = jnp.concatenate(strips, axis=1)
    p3_b, m3_b = shift(row_b, 0, -3), shift(row_b, 0, 3)
    from_minus_b = shift(jnp.concatenate([row_b, p3_b, m3_b[:, :512]], axis=1), 0, 1)
    from_plus_b = shift(jnp.concatenate([row_b, m3_b, p3_b[:, 512:]], axis=1), 0, -1)
    new_fragment = assemble(
        part1, part2, m1, m2, p1, p2, low, high, row_b, p3_b, m3_b, from_minus_b, from_plus_b
    )
    return (new_fragment, new_momentum)


def solution(mesh):
    in_specs = (P("replica", "shard", None), P("shard", None), P("shard", "replica"))
    out_specs = (P("shard", None), P("shard", "replica"))
    return jax.shard_map(shards, mesh=mesh, in_specs=in_specs, out_specs=out_specs, check_vma=False)
```

```python
import functools

import jax
import jax.numpy as jnp
import numpy as np
from jax import lax
from jax.experimental import pallas as pl
from jax.experimental.pallas import tpu as pltpu
from jax.sharding import PartitionSpec as P

epsilon = 1e-06
outer_rate = 0.7
momentum_decay = 0.9

NX, NZ = 4, 8
W = 256
ROWS_A = 128
ROWS_B = 128
BF, F32 = jnp.bfloat16, jnp.float32
VM = 32 * 2**20
GROUP = 8

Z_ORDER = (1, -2, 4, -1, 2, 0, 3, -3)
ANY = pl.BlockSpec(memory_space=pl.ANY)


def hadamard_blocks():
    index = np.arange(64)
    parity = np.zeros((64, 64), np.int64)
    for bit in range(6):
        parity += (index[:, None] >> bit) & (index[None, :] >> bit) & 1
    signs = (1 - 2 * (parity % 2)).astype(np.float32)
    return np.kron(np.eye(2, dtype=np.float32), signs) / 8.0


def params(**kw):
    return pltpu.CompilerParams(vmem_limit_bytes=VM, **kw)


def cost(flops, nbytes):
    return pl.CostEstimate(flops=flops, bytes_accessed=nbytes, transcendentals=0)


def position():
    replica = lax.axis_index("replica")
    return replica // NZ, lax.rem(replica, NZ)


def shift(value, dx, dz):
    pairs = [
        (x * NZ + z, (x + dx) % NX * NZ + (z + dz) % NZ) for x in range(NX) for z in range(NZ)
    ]
    return lax.ppermute(value, "replica", pairs)


def column_of(x, z, dx, dz):
    block = lax.rem(x + dx + NX, NX) * NZ + lax.rem(z + dz + NZ, NZ)
    return pl.multiple_of(block * W, W)


def tables():
    row = lax.broadcasted_iota(jnp.int32, (256, 256), 0)
    column = lax.broadcasted_iota(jnp.int32, (256, 256), 1)
    same = (row >> 6) == (column >> 6)
    bits = row & column & 63
    bits = bits ^ (bits >> 3)
    odd = (bits ^ (bits >> 1) ^ (bits >> 2)) & 1
    turn = jnp.where(same, (1 - 2 * odd).astype(F32) * 0.125, 0.0).astype(BF)
    mean4 = jnp.where(same, 4.0 / 64.0, 0.0).astype(BF)
    return turn, mean4


def contribute_kernel(jobs, after, local, base, *rest):
    n_out = sum(len(outs) + (own is not None) for _, _, _, outs, own in jobs)
    rest = rest[after:]
    out_refs, rest = list(rest[:n_out]), rest[n_out:]
    turn_ref, mean_ref, sem = rest[-3:]
    x, z = position()
    fetches = []
    k = 0
    for job, (row0, rows, slots, _, _) in enumerate(jobs):
        local_in, base_in = rest[2 * job : 2 * job + 2]
        for i, (dx, dz) in enumerate(slots):
            column = pl.ds(column_of(x, z, dx, dz), W)
            row = pl.ds(row0, rows)
            pair = (
                pltpu.make_async_copy(local.at[0, row, column], local_in.at[i], sem.at[0, k]),
                pltpu.make_async_copy(base.at[row, column], base_in.at[i], sem.at[1, k]),
            )
            for copy in pair:
                copy.start()
            fetches.append(pair)
            k += 1
    turn_ref[...], mean_ref[...] = tables()
    k = 0
    for job, (_, rows, slots, outs, own) in enumerate(jobs):
        local_in, base_in = rest[2 * job : 2 * job + 2]
        heads = [(out_refs.pop(0), count) for count in outs]
        places = [(ref, j) for ref, count in heads for j in range(count)]
        for i in range(0, len(slots), GROUP):
            group = min(GROUP, len(slots) - i)
            for pair in fetches[k : k + group]:
                for copy in pair:
                    copy.wait()
            k += group
            height = group * rows
            pseudo = base_in[i : i + group] - local_in[i : i + group]
            pseudo = pseudo.reshape(height, W)
            rotated = jnp.dot(pseudo, turn_ref[...], preferred_element_type=F32)
            power = jnp.dot(pseudo * pseudo, mean_ref[...], preferred_element_type=F32)
            power = power + 4.0 * epsilon
            limit = power * lax.rsqrt(power)
            value = jnp.minimum(jnp.maximum(rotated, -limit), limit).astype(BF)
            for g in range(group):
                out, j = places[i + g]
                out[:, pl.ds(j * W, W)] = value[g * rows : (g + 1) * rows]
        if own is not None:
            out_refs.pop(0)[...] = base_in[own]


def contribute(jobs, local, base, *after):
    n = sum(len(slots) for _, _, slots, _, _ in jobs)
    shapes, scratch = [], []
    for _, rows, slots, outs, own in jobs:
        for count in outs + (() if own is None else (1,)):
            shapes.append(jax.ShapeDtypeStruct((rows, count * W), BF))
        scratch += [pltpu.VMEM((len(slots), rows, W), BF)] * 2
    size = sum(rows * len(slots) * W for _, rows, slots, _, _ in jobs)
    return pl.pallas_call(
        functools.partial(contribute_kernel, jobs, len(after)),
        out_shape=shapes,
        in_specs=[pl.BlockSpec(memory_space=pltpu.HBM)] * 2 + [ANY] * len(after),
        out_specs=[pl.BlockSpec(memory_space=pltpu.VMEM)] * len(shapes),
        scratch_shapes=scratch
        + [
            pltpu.VMEM((256, 256), BF),
            pltpu.VMEM((256, 256), BF),
            pltpu.SemaphoreType.DMA((2, n)),
        ],
        compiler_params=params(),
        cost_estimate=cost(size * 1024, size * 6),
        name="contribute",
    )(local, base, *after)


def call(kernel, outs, *args, after=(), nbytes=2**20, name=None):
    n, skip = len(args), len(after)

    def body(*refs):
        kernel(*refs[:n], *refs[n + skip :])

    return pl.pallas_call(
        body,
        out_shape=[jax.ShapeDtypeStruct(s, d) for s, d in outs],
        in_specs=[pl.BlockSpec(memory_space=pltpu.VMEM)] * n + [ANY] * skip,
        out_specs=[pl.BlockSpec(memory_space=pltpu.VMEM)] * len(outs),
        compiler_params=params(),
        cost_estimate=cost(nbytes, nbytes),
        name=name,
    )(*args, *after)


def join(groups, *args, after=(), name=None):
    def kernel(*refs):
        for out, group in zip(refs[len(args) :], groups):
            at = 0
            for k, start, size in group:
                out[:, pl.ds(at, size)] = refs[k][:, pl.ds(start, size)]
                at += size

    outs = [((args[0].shape[0], sum(size for _, _, size in group)), BF) for group in groups]
    return call(kernel, outs, *args, after=after, name=name)


def f(ref, start, size):
    return ref[:, pl.ds(start, size)].astype(F32)


def relay_x_kernel(near_p, near_m, low, high, to_p, to_m):
    to_p[:, pl.ds(0, 1024)] = (f(near_p, 0, 1024) + f(low, 0, 1024)).astype(BF)
    to_p[:, pl.ds(1024, 1024)] = near_p[:, pl.ds(1024, 1024)]
    to_m[:, pl.ds(0, 1024)] = near_m[:, pl.ds(0, 1024)]
    to_m[:, pl.ds(1024, 1024)] = (f(near_m, 1024, 1024) + f(high, 0, 1024)).astype(BF)


def sum_x_kernel(own, r1, r2, *outs):
    start = 0
    for out in outs:
        size = out.shape[1]
        total = f(own, start, size) + f(r1, start, size) + f(r2, start, size)
        out[...] = total.astype(out.dtype)
        start += size


def relay_kernel(w, keep3p, keep3m, from_minus, from_plus, to3p, to3m):
    h = w // 2
    to3p[:, pl.ds(0, h)] = (
        f(keep3p, 0, h) + f(from_plus, h + w, h) + f(from_minus, 2 * w, h)
    ).astype(BF)
    to3p[:, pl.ds(h, h)] = (f(keep3p, h, h) + f(from_plus, 2 * w, h)).astype(BF)
    to3m[:, pl.ds(0, h)] = (f(keep3m, 0, h) + f(from_minus, w, h)).astype(BF)
    to3m[:, pl.ds(h, h)] = (f(keep3m, h, h) + f(from_minus, w + h, h) + f(from_plus, 0, h)).astype(
        BF
    )


def near(w, keep0, from_minus, from_plus, r3p, r3m, start, size):
    return (f(keep0, start, size) + f(from_minus, start, size)) + (
        f(from_plus, w // 2 + start, size) + f(r3p, start, size) + f(r3m, start, size)
    )


def sum_z_kernel(keep0, from_minus, from_plus, r3p, r3m, own, s1, s2, s3):
    for k, out in enumerate((own, s1, s2, s3)):
        out[...] = near(NX * W, keep0, from_minus, from_plus, r3p, r3m, k * W, W).astype(out.dtype)


def finish(summed, base, momentum, table, new_momentum, shard):
    for half in range(2):
        lanes = pl.ds(half * 128, 128)
        outer_grad = jnp.dot(
            summed[:, half * 128 : half * 128 + 128] * (1.0 / 32.0),
            table[...],
            precision=lax.Precision.HIGHEST,
            preferred_element_type=F32,
        )
        moved = momentum_decay * momentum[:, lanes] + outer_grad
        new_momentum[:, lanes] = moved
        updated = base[:, lanes].astype(F32) - outer_rate * (outer_grad + momentum_decay * moved)
        shard[:, lanes] = updated.astype(BF)


def update_a_kernel(keep0, from_minus, from_plus, r3p, r3m, *rest):
    finish(near(W, keep0, from_minus, from_plus, r3p, r3m, 0, W), *rest)


def update_b_kernel(own, b1, b2, b3, *rest):
    summed = (own[...] + b1[...].astype(F32)) + (b2[...].astype(F32) + b3[...].astype(F32))
    finish(summed, *rest)


def update(kernel, base, momentum, *args, after=()):
    table = jnp.asarray(hadamard_blocks(), F32)
    outs = [(momentum.shape, F32), (momentum.shape, BF)]
    return call(kernel, outs, *args, base, momentum, table, after=after, name="update")


LOW = ((0, 256, 0, 0), (256, 256, 3, 0), (512, 256, -3, 0), (768, 256, -1, 0))
HIGH = ((0, 256, 2, 0), (256, 128, 4, 0), (384, 256, 1, 0), (640, 256, -2, 0), (896, 128, 4, 128))
WHOLE = LOW + tuple((1024 + start, width, dz, inner) for start, width, dz, inner in HIGH)
ONE = ((0, 4, 0, 0),)
FROM_MINUS = ((0, 4, -1, 0), (1024, 4, 2, 0), (2048, 2, 4, 0))
FROM_PLUS = ((0, 4, 1, 0), (1024, 4, -2, 0), (2048, 2, 4, 2))


def assemble_kernel(plan, *refs):
    sources, out, sem = refs[: len(plan)], refs[-2], refs[-1]
    x, z = position()
    copies = []

    def put(source, start, width, row, dx, dz, inner):
        column = column_of(x, z, dx, dz) + inner
        column = pl.ds(pl.multiple_of(column, 128), width)
        k = len(copies)
        copy = pltpu.make_async_copy(source.at[:, pl.ds(start, width)], out.at[row, column], sem.at[k])
        copy.start()
        copies.append(copy)

    for source, (rows_b, shifted, pieces) in zip(sources, plan):
        if rows_b:
            for start, parts, dz, first in pieces:
                for k in range(parts):
                    row = pl.ds(ROWS_A, ROWS_B)
                    put(source, start + k * W, W, row, -(first + k), dz + shifted, 0)
        else:
            for start, width, dz, inner in pieces:
                put(source, start, width, pl.ds(0, ROWS_A), shifted, dz, inner)
    for copy in copies:
        copy.wait()


def assemble(plan, *blocks):
    aliases = {len(plan): 0} if len(blocks) > len(plan) else {}
    return pl.pallas_call(
        functools.partial(assemble_kernel, plan),
        out_shape=jax.ShapeDtypeStruct((ROWS_A + ROWS_B, NX * NZ * W), BF),
        in_specs=[ANY] * len(blocks),
        out_specs=ANY,
        scratch_shapes=[pltpu.SemaphoreType.DMA((80,))],
        input_output_aliases=aliases,
        compiler_params=params(),
        cost_estimate=cost(0, 2**22),
        name="assemble",
    )(*blocks)


def shards(local, base, momentum):
    z_a, z_b = Z_ORDER[:5], Z_ORDER[5:]
    local = pltpu.with_memory_space_constraint(local, pltpu.HBM)
    base = pltpu.with_memory_space_constraint(base, pltpu.HBM)

    far = tuple((2, dz) for dz in Z_ORDER)
    far_low, far_high = contribute(((0, ROWS_A, far, (4, 4), None),), local, base)
    low, high = shift(far_low, 1, 0), shift(far_high, -1, 0)
    sent_b = tuple((dx, dz) for dz in z_a for dx in range(NX))
    plus_b, minus_b = contribute(
        ((ROWS_A, ROWS_B, sent_b, (10, 10), None),), local, base, far_low
    )
    from_minus_b, from_plus_b = shift(plus_b, 0, 1), shift(minus_b, 0, -1)
    near_x = tuple((dx, dz) for dx in (1, -1) for dz in Z_ORDER)
    near_p, near_m = contribute(((0, ROWS_A, near_x, (8, 8), None),), local, base)

    wide = (ROWS_A, 2048)
    to_p, to_m = call(relay_x_kernel, [(wide, BF)] * 2, near_p, near_m, low, high, name="relay_x")
    r_p, r_m = shift(to_p, 1, 0), shift(to_m, -1, 0)
    own_x = tuple((0, dz) for dz in Z_ORDER)
    kept_b = tuple((dx, dz) for dz in z_b for dx in range(NX))
    own_x, base_a, keep0_b, keep3p_b, keep3m_b, base_b = contribute(
        ((0, ROWS_A, own_x, (8,), 5), (ROWS_A, ROWS_B, kept_b, (4, 4, 4), 0)), local, base
    )

    half = (ROWS_B, NX * W)
    to3p_b, to3m_b = call(
        functools.partial(relay_kernel, NX * W), [(half, BF), (half, BF)],
        keep3p_b, keep3m_b, from_minus_b, from_plus_b, name="relay_b",
    )
    r3p_b, r3m_b = shift(to3p_b, 0, 3), shift(to3m_b, 0, -3)

    strip, group = (ROWS_A, W), (ROWS_A, 640)
    plus_a, minus_a, keep0, keep3p, keep3m = call(
        sum_x_kernel, [(group, BF), (group, BF)] + [(strip, F32)] * 3, own_x, r_p, r_m,
        name="sum_a",
    )
    from_minus, from_plus = shift(plus_a, 0, 1), shift(minus_a, 0, -1)
    to3p, to3m = call(
        functools.partial(relay_kernel, W), [(strip, BF), (strip, BF)],
        keep3p, keep3m, from_minus, from_plus, name="relay_a",
    )
    r3p, r3m = shift(to3p, 0, 3), shift(to3m, 0, -3)

    strip = (ROWS_B, W)
    own, s1, s2, s3 = call(
        sum_z_kernel, [(strip, F32), (strip, BF), (strip, BF), (strip, BF)],
        keep0_b, from_minus_b, from_plus_b, r3p_b, r3m_b, after=(to3p,), name="sum_b",
    )
    b1, b2, b3 = shift(s1, 1, 0), shift(s2, 2, 0), shift(s3, 3, 0)

    momentum_a, own_a = update(
        update_a_kernel, base_a, momentum[:ROWS_A], keep0, from_minus, from_plus, r3p, r3m
    )
    p3, m3 = shift(own_a, 0, -3), shift(own_a, 0, 3)
    momentum_b, own_b = update(
        update_b_kernel, base_b, momentum[ROWS_A:], own, b1, b2, b3, after=(own_a,)
    )
    b1, b2, b3 = [shift(own_b, e, 0) for e in (1, 2, 3)]
    plus_a, minus_a = join(
        (((0, 0, W), (1, 0, W), (2, 0, 128)), ((0, 0, W), (2, 0, W), (1, 128, 128))),
        own_a, p3, m3, after=(own_b,), name="join_a",
    )
    from_minus, from_plus = shift(plus_a, 0, 1), shift(minus_a, 0, -1)
    (row_b,) = join(
        (((0, 0, W), (1, 0, W), (2, 0, W), (3, 0, W)),),
        own_b, b1, b2, b3, after=(plus_a,), name="join_b",
    )
    p3_b, m3_b = shift(row_b, 0, -3), shift(row_b, 0, 3)
    (row_a,) = join(
        (((0, 0, W), (1, 0, W), (2, 0, W), (3, 0, 640), (4, 0, 640)),),
        own_a, p3, m3, from_minus, from_plus, after=(row_b,), name="join_row_a",
    )
    m1, p1 = shift(row_a, 1, 0), shift(row_a, -1, 0)
    plus_b, minus_b = join(
        (((0, 0, 1024), (1, 0, 1024), (2, 0, 512)), ((0, 0, 1024), (2, 0, 1024), (1, 512, 512))),
        row_b, p3_b, m3_b, after=(row_a,), name="join_row_b",
    )
    from_minus_b, from_plus_b = shift(plus_b, 0, 1), shift(minus_b, 0, -1)
    low, high = join(
        (((0, 0, 1024),), ((1, 1024, 1024),)), m1, p1, after=(plus_b,), name="relay_row_a"
    )
    low, high = shift(low, 1, 0), shift(high, -1, 0)
    new_momentum = jnp.concatenate([momentum_a, momentum_b], axis=0)
    early = ((0, 0, WHOLE), (0, -1, WHOLE), (0, 1, WHOLE), (1, 0, ONE), (1, 3, ONE), (1, -3, ONE))
    late = ((0, 2, LOW), (0, 2, HIGH), (1, 0, FROM_MINUS), (1, 0, FROM_PLUS))
    partial = assemble(early, row_a, m1, p1, row_b, p3_b, m3_b)
    new_fragment = assemble(late, low, high, from_minus_b, from_plus_b, partial)
    return (new_fragment, new_momentum)


def solution(mesh):
    in_specs = (P("replica", "shard", None), P("shard", None), P("shard", "replica"))
    out_specs = (P("shard", None), P("shard", "replica"))
    return jax.shard_map(shards, mesh=mesh, in_specs=in_specs, out_specs=out_specs, check_vma=False)
```

```python
import functools

import jax
import jax.numpy as jnp
import numpy as np
from jax import lax
from jax.experimental import pallas as pl
from jax.experimental.pallas import tpu as pltpu
from jax.sharding import PartitionSpec as P

epsilon = 1e-06
outer_rate = 0.7
momentum_decay = 0.9

NX, NZ = 4, 8
W = 256
ROWS_A = 128
ROWS_B = 128
BF, F32 = jnp.bfloat16, jnp.float32
VM = 32 * 2**20
GROUP = 8

Z_ORDER = (1, -2, 4, -1, 2, 0, 3, -3)
ANY = pl.BlockSpec(memory_space=pl.ANY)


def hadamard_blocks():
    index = np.arange(64)
    parity = np.zeros((64, 64), np.int64)
    for bit in range(6):
        parity += (index[:, None] >> bit) & (index[None, :] >> bit) & 1
    signs = (1 - 2 * (parity % 2)).astype(np.float32)
    return np.kron(np.eye(2, dtype=np.float32), signs) / 8.0


def params(**kw):
    return pltpu.CompilerParams(vmem_limit_bytes=VM, **kw)


def cost(flops, nbytes):
    return pl.CostEstimate(flops=flops, bytes_accessed=nbytes, transcendentals=0)


def position():
    replica = lax.axis_index("replica")
    return replica // NZ, lax.rem(replica, NZ)


def shift(value, dx, dz):
    pairs = [
        (x * NZ + z, (x + dx) % NX * NZ + (z + dz) % NZ) for x in range(NX) for z in range(NZ)
    ]
    return lax.ppermute(value, "replica", pairs)


def column_of(x, z, dx, dz):
    block = lax.rem(x + dx + NX, NX) * NZ + lax.rem(z + dz + NZ, NZ)
    return pl.multiple_of(block * W, W)


def tables():
    row = lax.broadcasted_iota(jnp.int32, (256, 256), 0)
    column = lax.broadcasted_iota(jnp.int32, (256, 256), 1)
    same = (row >> 6) == (column >> 6)
    bits = row & column & 63
    bits = bits ^ (bits >> 3)
    odd = (bits ^ (bits >> 1) ^ (bits >> 2)) & 1
    turn = jnp.where(same, (1 - 2 * odd).astype(F32) * 0.125, 0.0).astype(BF)
    mean4 = jnp.where(same, 4.0 / 64.0, 0.0).astype(BF)
    return turn, mean4


def contribute_kernel(jobs, after, local, base, *rest):
    n_out = sum(len(outs) + (own is not None) for _, _, _, outs, own in jobs)
    rest = rest[after:]
    out_refs, rest = list(rest[:n_out]), rest[n_out:]
    turn_ref, mean_ref, sem = rest[-3:]
    x, z = position()
    fetches = []
    k = 0
    for job, (row0, rows, slots, _, _) in enumerate(jobs):
        local_in, base_in = rest[2 * job : 2 * job + 2]
        for i, (dx, dz) in enumerate(slots):
            column = pl.ds(column_of(x, z, dx, dz), W)
            row = pl.ds(row0, rows)
            pair = (
                pltpu.make_async_copy(local.at[0, row, column], local_in.at[i], sem.at[0, k]),
                pltpu.make_async_copy(base.at[row, column], base_in.at[i], sem.at[1, k]),
            )
            for copy in pair:
                copy.start()
            fetches.append(pair)
            k += 1
    turn_ref[...], mean_ref[...] = tables()
    k = 0
    for job, (_, rows, slots, outs, own) in enumerate(jobs):
        local_in, base_in = rest[2 * job : 2 * job + 2]
        heads = [(out_refs.pop(0), count) for count in outs]
        places = [(ref, j) for ref, count in heads for j in range(count)]
        for i in range(0, len(slots), GROUP):
            group = min(GROUP, len(slots) - i)
            for pair in fetches[k : k + group]:
                for copy in pair:
                    copy.wait()
            k += group
            height = group * rows
            pseudo = base_in[i : i + group] - local_in[i : i + group]
            pseudo = pseudo.reshape(height, W)
            rotated = jnp.dot(pseudo, turn_ref[...], preferred_element_type=F32)
            power = jnp.dot(pseudo * pseudo, mean_ref[...], preferred_element_type=F32)
            power = power + 4.0 * epsilon
            limit = power * lax.rsqrt(power)
            value = jnp.minimum(jnp.maximum(rotated, -limit), limit).astype(BF)
            for g in range(group):
                out, j = places[i + g]
                out[:, pl.ds(j * W, W)] = value[g * rows : (g + 1) * rows]
        if own is not None:
            out_refs.pop(0)[...] = base_in[own]


def contribute(jobs, local, base, *after):
    n = sum(len(slots) for _, _, slots, _, _ in jobs)
    shapes, scratch = [], []
    for _, rows, slots, outs, own in jobs:
        for count in outs + (() if own is None else (1,)):
            shapes.append(jax.ShapeDtypeStruct((rows, count * W), BF))
        scratch += [pltpu.VMEM((len(slots), rows, W), BF)] * 2
    size = sum(rows * len(slots) * W for _, rows, slots, _, _ in jobs)
    return pl.pallas_call(
        functools.partial(contribute_kernel, jobs, len(after)),
        out_shape=shapes,
        in_specs=[pl.BlockSpec(memory_space=pltpu.HBM)] * 2 + [ANY] * len(after),
        out_specs=[pl.BlockSpec(memory_space=pltpu.VMEM)] * len(shapes),
        scratch_shapes=scratch
        + [
            pltpu.VMEM((256, 256), BF),
            pltpu.VMEM((256, 256), BF),
            pltpu.SemaphoreType.DMA((2, n)),
        ],
        compiler_params=params(),
        cost_estimate=cost(size * 1024, size * 6),
        name="contribute",
    )(local, base, *after)


def call(kernel, outs, *args, after=(), nbytes=2**20, name=None):
    n, skip = len(args), len(after)

    def body(*refs):
        kernel(*refs[:n], *refs[n + skip :])

    return pl.pallas_call(
        body,
        out_shape=[jax.ShapeDtypeStruct(s, d) for s, d in outs],
        in_specs=[pl.BlockSpec(memory_space=pltpu.VMEM)] * n + [ANY] * skip,
        out_specs=[pl.BlockSpec(memory_space=pltpu.VMEM)] * len(outs),
        compiler_params=params(),
        cost_estimate=cost(nbytes, nbytes),
        name=name,
    )(*args, *after)


def join(groups, *args, after=(), name=None):
    def kernel(*refs):
        for out, group in zip(refs[len(args) :], groups):
            at = 0
            for k, start, size in group:
                out[:, pl.ds(at, size)] = refs[k][:, pl.ds(start, size)]
                at += size

    outs = [((args[0].shape[0], sum(size for _, _, size in group)), BF) for group in groups]
    return call(kernel, outs, *args, after=after, name=name)


def f(ref, start, size):
    return ref[:, pl.ds(start, size)].astype(F32)


def relay_x_kernel(near_p, near_m, low, high, to_p, to_m):
    to_p[:, pl.ds(0, 1024)] = (f(near_p, 0, 1024) + f(low, 0, 1024)).astype(BF)
    to_p[:, pl.ds(1024, 1024)] = near_p[:, pl.ds(1024, 1024)]
    to_m[:, pl.ds(0, 1024)] = near_m[:, pl.ds(0, 1024)]
    to_m[:, pl.ds(1024, 1024)] = (f(near_m, 1024, 1024) + f(high, 0, 1024)).astype(BF)


def sum_x_kernel(own, r1, r2, *outs):
    start = 0
    for out in outs:
        size = out.shape[1]
        total = f(own, start, size) + f(r1, start, size) + f(r2, start, size)
        out[...] = total.astype(out.dtype)
        start += size


def relay_kernel(w, keep3p, keep3m, from_minus, from_plus, to3p, to3m):
    h = w // 2
    to3p[:, pl.ds(0, h)] = (
        f(keep3p, 0, h) + f(from_plus, h + w, h) + f(from_minus, 2 * w, h)
    ).astype(BF)
    to3p[:, pl.ds(h, h)] = (f(keep3p, h, h) + f(from_plus, 2 * w, h)).astype(BF)
    to3m[:, pl.ds(0, h)] = (f(keep3m, 0, h) + f(from_minus, w, h)).astype(BF)
    to3m[:, pl.ds(h, h)] = (f(keep3m, h, h) + f(from_minus, w + h, h) + f(from_plus, 0, h)).astype(
        BF
    )


def near(w, keep0, from_minus, from_plus, r3p, r3m, start, size):
    return (f(keep0, start, size) + f(from_minus, start, size)) + (
        f(from_plus, w // 2 + start, size) + f(r3p, start, size) + f(r3m, start, size)
    )


def sum_z_kernel(keep0, from_minus, from_plus, r3p, r3m, own, s1, s2, s3):
    for k, out in enumerate((own, s1, s2, s3)):
        out[...] = near(NX * W, keep0, from_minus, from_plus, r3p, r3m, k * W, W).astype(out.dtype)


def finish(summed, base, momentum, table, new_momentum, shard):
    for half in range(2):
        lanes = pl.ds(half * 128, 128)
        outer_grad = jnp.dot(
            summed[:, half * 128 : half * 128 + 128] * (1.0 / 32.0),
            table[...],
            precision=lax.Precision.HIGHEST,
            preferred_element_type=F32,
        )
        moved = momentum_decay * momentum[:, lanes] + outer_grad
        new_momentum[:, lanes] = moved
        updated = base[:, lanes].astype(F32) - outer_rate * (outer_grad + momentum_decay * moved)
        shard[:, lanes] = updated.astype(BF)


def update_a_kernel(keep0, from_minus, from_plus, r3p, r3m, *rest):
    finish(near(W, keep0, from_minus, from_plus, r3p, r3m, 0, W), *rest)


def update_b_kernel(own, b1, b2, b3, *rest):
    summed = (own[...] + b1[...].astype(F32)) + (b2[...].astype(F32) + b3[...].astype(F32))
    finish(summed, *rest)


def update(kernel, base, momentum, *args, after=()):
    table = jnp.asarray(hadamard_blocks(), F32)
    outs = [(momentum.shape, F32), (momentum.shape, BF)]
    return call(kernel, outs, *args, base, momentum, table, after=after, name="update")


LOW = ((0, 256, 0, 0), (256, 256, 3, 0), (512, 256, -3, 0), (768, 256, -1, 0))
HIGH = ((0, 256, 2, 0), (256, 128, 4, 0), (384, 256, 1, 0), (640, 256, -2, 0), (896, 128, 4, 128))
WHOLE = LOW + tuple((1024 + start, width, dz, inner) for start, width, dz, inner in HIGH)
ONE = ((0, 4, 0, 0),)
FROM_MINUS = ((0, 4, -1, 0), (1024, 4, 2, 0), (2048, 2, 4, 0))
FROM_PLUS = ((0, 4, 1, 0), (1024, 4, -2, 0), (2048, 2, 4, 2))


def assemble_kernel(plan, *refs):
    sources, out, sem = refs[: len(plan)], refs[-2], refs[-1]
    x, z = position()
    copies = []

    def put(source, start, width, row, dx, dz, inner):
        column = column_of(x, z, dx, dz) + inner
        column = pl.ds(pl.multiple_of(column, 128), width)
        k = len(copies)
        copy = pltpu.make_async_copy(source.at[:, pl.ds(start, width)], out.at[row, column], sem.at[k])
        copy.start()
        copies.append(copy)

    for source, (rows_b, shifted, pieces) in zip(sources, plan):
        if rows_b:
            for start, parts, dz, first in pieces:
                for k in range(parts):
                    row = pl.ds(ROWS_A, ROWS_B)
                    put(source, start + k * W, W, row, -(first + k), dz + shifted, 0)
        else:
            for start, width, dz, inner in pieces:
                put(source, start, width, pl.ds(0, ROWS_A), shifted, dz, inner)
    for copy in copies:
        copy.wait()


def assemble(plan, *blocks):
    aliases = {len(plan): 0} if len(blocks) > len(plan) else {}
    return pl.pallas_call(
        functools.partial(assemble_kernel, plan),
        out_shape=jax.ShapeDtypeStruct((ROWS_A + ROWS_B, NX * NZ * W), BF),
        in_specs=[ANY] * len(blocks),
        out_specs=ANY,
        scratch_shapes=[pltpu.SemaphoreType.DMA((80,))],
        input_output_aliases=aliases,
        compiler_params=params(),
        cost_estimate=cost(0, 2**22),
        name="assemble",
    )(*blocks)


def shards(local, base, momentum):
    z_a, z_b = Z_ORDER[:5], Z_ORDER[5:]
    local = pltpu.with_memory_space_constraint(local, pltpu.HBM)
    base = pltpu.with_memory_space_constraint(base, pltpu.HBM)

    far = tuple((2, dz) for dz in Z_ORDER)
    far_low, far_high = contribute(((0, ROWS_A, far, (4, 4), None),), local, base)
    low, high = shift(far_low, 1, 0), shift(far_high, -1, 0)
    sent_b = tuple((dx, dz) for dz in z_a for dx in range(NX))
    plus_b, minus_b = contribute(
        ((ROWS_A, ROWS_B, sent_b, (10, 10), None),), local, base, far_low
    )
    from_minus_b, from_plus_b = shift(plus_b, 0, 1), shift(minus_b, 0, -1)
    near_x = tuple((dx, dz) for dx in (1, -1) for dz in Z_ORDER)
    near_p, near_m = contribute(((0, ROWS_A, near_x, (8, 8), None),), local, base)

    wide = (ROWS_A, 2048)
    to_p, to_m = call(relay_x_kernel, [(wide, BF)] * 2, near_p, near_m, low, high, name="relay_x")
    r_p, r_m = shift(to_p, 1, 0), shift(to_m, -1, 0)
    own_x = tuple((0, dz) for dz in Z_ORDER)
    kept_b = tuple((dx, dz) for dz in z_b for dx in range(NX))
    own_x, base_a, keep0_b, keep3p_b, keep3m_b, base_b = contribute(
        ((0, ROWS_A, own_x, (8,), 5), (ROWS_A, ROWS_B, kept_b, (4, 4, 4), 0)), local, base
    )

    half = (ROWS_B, NX * W)
    to3p_b, to3m_b = call(
        functools.partial(relay_kernel, NX * W), [(half, BF), (half, BF)],
        keep3p_b, keep3m_b, from_minus_b, from_plus_b, name="relay_b",
    )
    r3p_b, r3m_b = shift(to3p_b, 0, 3), shift(to3m_b, 0, -3)

    strip, group = (ROWS_A, W), (ROWS_A, 640)
    plus_a, minus_a, keep0, keep3p, keep3m = call(
        sum_x_kernel, [(group, BF), (group, BF)] + [(strip, F32)] * 3, own_x, r_p, r_m,
        name="sum_a",
    )
    from_minus, from_plus = shift(plus_a, 0, 1), shift(minus_a, 0, -1)
    to3p, to3m = call(
        functools.partial(relay_kernel, W), [(strip, BF), (strip, BF)],
        keep3p, keep3m, from_minus, from_plus, name="relay_a",
    )
    r3p, r3m = shift(to3p, 0, 3), shift(to3m, 0, -3)

    strip = (ROWS_B, W)
    own, s1, s2, s3 = call(
        sum_z_kernel, [(strip, F32), (strip, BF), (strip, BF), (strip, BF)],
        keep0_b, from_minus_b, from_plus_b, r3p_b, r3m_b, after=(to3p,), name="sum_b",
    )
    b1, b2, b3 = shift(s1, 1, 0), shift(s2, 2, 0), shift(s3, 3, 0)

    momentum_a, own_a = update(
        update_a_kernel, base_a, momentum[:ROWS_A], keep0, from_minus, from_plus, r3p, r3m
    )
    p3, m3 = shift(own_a, 0, -3), shift(own_a, 0, 3)
    momentum_b, own_b = update(
        update_b_kernel, base_b, momentum[ROWS_A:], own, b1, b2, b3, after=(own_a,)
    )
    b1, b2, b3 = [shift(own_b, e, 0) for e in (1, 2, 3)]
    plus_a, minus_a = join(
        (((0, 0, W), (1, 0, W), (2, 0, 128)), ((0, 0, W), (2, 0, W), (1, 128, 128))),
        own_a, p3, m3, after=(own_b,), name="join_a",
    )
    from_minus, from_plus = shift(plus_a, 0, 1), shift(minus_a, 0, -1)
    (row_b,) = join(
        (((0, 0, W), (1, 0, W), (2, 0, W), (3, 0, W)),),
        own_b, b1, b2, b3, after=(plus_a,), name="join_b",
    )
    p3_b, m3_b = shift(row_b, 0, -3), shift(row_b, 0, 3)
    (row_a,) = join(
        (((0, 0, W), (1, 0, W), (2, 0, W), (3, 0, 640), (4, 0, 640)),),
        own_a, p3, m3, from_minus, from_plus, after=(row_b,), name="join_row_a",
    )
    m1, p1 = shift(row_a, 1, 0), shift(row_a, -1, 0)
    plus_b, minus_b = join(
        (((0, 0, 1024), (1, 0, 1024), (2, 0, 512)), ((0, 0, 1024), (2, 0, 1024), (1, 512, 512))),
        row_b, p3_b, m3_b, after=(row_a,), name="join_row_b",
    )
    from_minus_b, from_plus_b = shift(plus_b, 0, 1), shift(minus_b, 0, -1)
    low, high = join(
        (((0, 0, 1024),), ((1, 1024, 1024),)), m1, p1, name="relay_row_a"
    )
    low, high = shift(low, 1, 0), shift(high, -1, 0)
    new_momentum = jnp.concatenate([momentum_a, momentum_b], axis=0)
    early = ((0, 0, WHOLE), (0, -1, WHOLE), (0, 1, WHOLE), (1, 0, ONE), (1, 3, ONE), (1, -3, ONE))
    late = ((0, 2, LOW), (0, 2, HIGH), (1, 0, FROM_MINUS), (1, 0, FROM_PLUS))
    partial = assemble(early, row_a, m1, p1, row_b, p3_b, m3_b)
    new_fragment = assemble(late, low, high, from_minus_b, from_plus_b, partial)
    return (new_fragment, new_momentum)


def solution(mesh):
    in_specs = (P("replica", "shard", None), P("shard", None), P("shard", "replica"))
    out_specs = (P("shard", None), P("shard", "replica"))
    return jax.shard_map(shards, mesh=mesh, in_specs=in_specs, out_specs=out_specs, check_vma=False)
```

```python
import functools

import jax
import jax.numpy as jnp
import numpy as np
from jax import lax
from jax.experimental import pallas as pl
from jax.experimental.pallas import tpu as pltpu
from jax.sharding import PartitionSpec as P

epsilon = 1e-06
outer_rate = 0.7
momentum_decay = 0.9

NX, NZ = 4, 8
W = 256
ROWS_A = 128
ROWS_B = 128
BF, F32 = jnp.bfloat16, jnp.float32
VM = 32 * 2**20
GROUP = 8

Z_ORDER = (1, -2, 4, -1, 2, 0, 3, -3)
ANY = pl.BlockSpec(memory_space=pl.ANY)


def hadamard_blocks():
    index = np.arange(64)
    parity = np.zeros((64, 64), np.int64)
    for bit in range(6):
        parity += (index[:, None] >> bit) & (index[None, :] >> bit) & 1
    signs = (1 - 2 * (parity % 2)).astype(np.float32)
    return np.kron(np.eye(2, dtype=np.float32), signs) / 8.0


def params(**kw):
    return pltpu.CompilerParams(vmem_limit_bytes=VM, **kw)


def cost(flops, nbytes):
    return pl.CostEstimate(flops=flops, bytes_accessed=nbytes, transcendentals=0)


def position():
    replica = lax.axis_index("replica")
    return replica // NZ, lax.rem(replica, NZ)


def shift(value, dx, dz):
    pairs = [
        (x * NZ + z, (x + dx) % NX * NZ + (z + dz) % NZ) for x in range(NX) for z in range(NZ)
    ]
    return lax.ppermute(value, "replica", pairs)


def column_of(x, z, dx, dz):
    block = lax.rem(x + dx + NX, NX) * NZ + lax.rem(z + dz + NZ, NZ)
    return pl.multiple_of(block * W, W)


def tables():
    row = lax.broadcasted_iota(jnp.int32, (256, 256), 0)
    column = lax.broadcasted_iota(jnp.int32, (256, 256), 1)
    same = (row >> 6) == (column >> 6)
    bits = row & column & 63
    bits = bits ^ (bits >> 3)
    odd = (bits ^ (bits >> 1) ^ (bits >> 2)) & 1
    turn = jnp.where(same, (1 - 2 * odd).astype(F32) * 0.125, 0.0).astype(BF)
    mean4 = jnp.where(same, 4.0 / 64.0, 0.0).astype(BF)
    return turn, mean4


def contribute_kernel(jobs, after, local, base, *rest):
    n_out = sum(len(outs) + (own is not None) for _, _, _, outs, own in jobs)
    rest = rest[after:]
    out_refs, rest = list(rest[:n_out]), rest[n_out:]
    turn_ref, mean_ref, sem = rest[-3:]
    x, z = position()
    fetches = []
    k = 0
    for job, (row0, rows, slots, _, _) in enumerate(jobs):
        local_in, base_in = rest[2 * job : 2 * job + 2]
        for i, (dx, dz) in enumerate(slots):
            column = pl.ds(column_of(x, z, dx, dz), W)
            row = pl.ds(row0, rows)
            pair = (
                pltpu.make_async_copy(local.at[0, row, column], local_in.at[i], sem.at[0, k]),
                pltpu.make_async_copy(base.at[row, column], base_in.at[i], sem.at[1, k]),
            )
            for copy in pair:
                copy.start()
            fetches.append(pair)
            k += 1
    turn_ref[...], mean_ref[...] = tables()
    k = 0
    for job, (_, rows, slots, outs, own) in enumerate(jobs):
        local_in, base_in = rest[2 * job : 2 * job + 2]
        heads = [(out_refs.pop(0), count) for count in outs]
        places = [(ref, j) for ref, count in heads for j in range(count)]
        for i in range(0, len(slots), GROUP):
            group = min(GROUP, len(slots) - i)
            for pair in fetches[k : k + group]:
                for copy in pair:
                    copy.wait()
            k += group
            height = group * rows
            pseudo = base_in[i : i + group] - local_in[i : i + group]
            pseudo = pseudo.reshape(height, W)
            rotated = jnp.dot(pseudo, turn_ref[...], preferred_element_type=F32)
            power = jnp.dot(pseudo * pseudo, mean_ref[...], preferred_element_type=F32)
            power = power + 4.0 * epsilon
            limit = power * lax.rsqrt(power)
            value = jnp.minimum(jnp.maximum(rotated, -limit), limit).astype(BF)
            for g in range(group):
                out, j = places[i + g]
                out[:, pl.ds(j * W, W)] = value[g * rows : (g + 1) * rows]
        if own is not None:
            out_refs.pop(0)[...] = base_in[own]


def contribute(jobs, local, base, *after):
    n = sum(len(slots) for _, _, slots, _, _ in jobs)
    shapes, scratch = [], []
    for _, rows, slots, outs, own in jobs:
        for count in outs + (() if own is None else (1,)):
            shapes.append(jax.ShapeDtypeStruct((rows, count * W), BF))
        scratch += [pltpu.VMEM((len(slots), rows, W), BF)] * 2
    size = sum(rows * len(slots) * W for _, rows, slots, _, _ in jobs)
    return pl.pallas_call(
        functools.partial(contribute_kernel, jobs, len(after)),
        out_shape=shapes,
        in_specs=[pl.BlockSpec(memory_space=pltpu.HBM)] * 2 + [ANY] * len(after),
        out_specs=[pl.BlockSpec(memory_space=pltpu.VMEM)] * len(shapes),
        scratch_shapes=scratch
        + [
            pltpu.VMEM((256, 256), BF),
            pltpu.VMEM((256, 256), BF),
            pltpu.SemaphoreType.DMA((2, n)),
        ],
        compiler_params=params(),
        cost_estimate=cost(size * 1024, size * 6),
        name="contribute",
    )(local, base, *after)


def call(kernel, outs, *args, after=(), nbytes=2**20, name=None):
    n, skip = len(args), len(after)

    def body(*refs):
        kernel(*refs[:n], *refs[n + skip :])

    return pl.pallas_call(
        body,
        out_shape=[jax.ShapeDtypeStruct(s, d) for s, d in outs],
        in_specs=[pl.BlockSpec(memory_space=pltpu.VMEM)] * n + [ANY] * skip,
        out_specs=[pl.BlockSpec(memory_space=pltpu.VMEM)] * len(outs),
        compiler_params=params(),
        cost_estimate=cost(nbytes, nbytes),
        name=name,
    )(*args, *after)


def join(groups, *args, after=(), name=None):
    def kernel(*refs):
        for out, group in zip(refs[len(args) :], groups):
            at = 0
            for k, start, size in group:
                out[:, pl.ds(at, size)] = refs[k][:, pl.ds(start, size)]
                at += size

    outs = [((args[0].shape[0], sum(size for _, _, size in group)), BF) for group in groups]
    return call(kernel, outs, *args, after=after, name=name)


def f(ref, start, size):
    return ref[:, pl.ds(start, size)].astype(F32)


def relay_x_kernel(near_p, near_m, low, high, to_p, to_m):
    to_p[:, pl.ds(0, 1024)] = (f(near_p, 0, 1024) + f(low, 0, 1024)).astype(BF)
    to_p[:, pl.ds(1024, 1024)] = near_p[:, pl.ds(1024, 1024)]
    to_m[:, pl.ds(0, 1024)] = near_m[:, pl.ds(0, 1024)]
    to_m[:, pl.ds(1024, 1024)] = (f(near_m, 1024, 1024) + f(high, 0, 1024)).astype(BF)


def sum_x_kernel(own, r1, r2, *outs):
    start = 0
    for out in outs:
        size = out.shape[1]
        total = f(own, start, size) + f(r1, start, size) + f(r2, start, size)
        out[...] = total.astype(out.dtype)
        start += size


def relay_kernel(w, keep3p, keep3m, from_minus, from_plus, to3p, to3m):
    h = w // 2
    to3p[:, pl.ds(0, h)] = (
        f(keep3p, 0, h) + f(from_plus, h + w, h) + f(from_minus, 2 * w, h)
    ).astype(BF)
    to3p[:, pl.ds(h, h)] = (f(keep3p, h, h) + f(from_plus, 2 * w, h)).astype(BF)
    to3m[:, pl.ds(0, h)] = (f(keep3m, 0, h) + f(from_minus, w, h)).astype(BF)
    to3m[:, pl.ds(h, h)] = (f(keep3m, h, h) + f(from_minus, w + h, h) + f(from_plus, 0, h)).astype(
        BF
    )


def near(w, keep0, from_minus, from_plus, r3p, r3m, start, size):
    return (f(keep0, start, size) + f(from_minus, start, size)) + (
        f(from_plus, w // 2 + start, size) + f(r3p, start, size) + f(r3m, start, size)
    )


def sum_z_kernel(keep0, from_minus, from_plus, r3p, r3m, own, s1, s2, s3):
    for k, out in enumerate((own, s1, s2, s3)):
        out[...] = near(NX * W, keep0, from_minus, from_plus, r3p, r3m, k * W, W).astype(out.dtype)


def finish(summed, base, momentum, table, new_momentum, shard):
    for half in range(2):
        lanes = pl.ds(half * 128, 128)
        outer_grad = jnp.dot(
            summed[:, half * 128 : half * 128 + 128] * (1.0 / 32.0),
            table[...],
            precision=lax.Precision.HIGHEST,
            preferred_element_type=F32,
        )
        moved = momentum_decay * momentum[:, lanes] + outer_grad
        new_momentum[:, lanes] = moved
        updated = base[:, lanes].astype(F32) - outer_rate * (outer_grad + momentum_decay * moved)
        shard[:, lanes] = updated.astype(BF)


def update_a_kernel(keep0, from_minus, from_plus, r3p, r3m, *rest):
    finish(near(W, keep0, from_minus, from_plus, r3p, r3m, 0, W), *rest)


def update_b_kernel(own, b1, b2, b3, *rest):
    summed = (own[...] + b1[...].astype(F32)) + (b2[...].astype(F32) + b3[...].astype(F32))
    finish(summed, *rest)


def update(kernel, base, momentum, *args, after=()):
    table = jnp.asarray(hadamard_blocks(), F32)
    outs = [(momentum.shape, F32), (momentum.shape, BF)]
    return call(kernel, outs, *args, base, momentum, table, after=after, name="update")


LOW = ((0, 256, 0, 0), (256, 256, 3, 0), (512, 256, -3, 0), (768, 256, -1, 0))
HIGH = ((0, 256, 2, 0), (256, 128, 4, 0), (384, 256, 1, 0), (640, 256, -2, 0), (896, 128, 4, 128))
WHOLE = LOW + tuple((1024 + start, width, dz, inner) for start, width, dz, inner in HIGH)
ONE = ((0, 4, 0, 0),)
FROM_MINUS = ((0, 4, -1, 0), (1024, 4, 2, 0), (2048, 2, 4, 0))
FROM_PLUS = ((0, 4, 1, 0), (1024, 4, -2, 0), (2048, 2, 4, 2))


def assemble_kernel(plan, *refs):
    sources, out, sem = refs[: len(plan)], refs[-2], refs[-1]
    x, z = position()
    copies = []

    def put(source, start, width, row, dx, dz, inner):
        column = column_of(x, z, dx, dz) + inner
        column = pl.ds(pl.multiple_of(column, 128), width)
        k = len(copies)
        copy = pltpu.make_async_copy(source.at[:, pl.ds(start, width)], out.at[row, column], sem.at[k])
        copy.start()
        copies.append(copy)

    for source, (rows_b, shifted, pieces) in zip(sources, plan):
        if rows_b:
            for start, parts, dz, first in pieces:
                for k in range(parts):
                    row = pl.ds(ROWS_A, ROWS_B)
                    put(source, start + k * W, W, row, -(first + k), dz + shifted, 0)
        else:
            for start, width, dz, inner in pieces:
                put(source, start, width, pl.ds(0, ROWS_A), shifted, dz, inner)
    for copy in copies:
        copy.wait()


def assemble(plan, *blocks):
    aliases = {len(plan): 0} if len(blocks) > len(plan) else {}
    return pl.pallas_call(
        functools.partial(assemble_kernel, plan),
        out_shape=jax.ShapeDtypeStruct((ROWS_A + ROWS_B, NX * NZ * W), BF),
        in_specs=[ANY] * len(blocks),
        out_specs=ANY,
        scratch_shapes=[pltpu.SemaphoreType.DMA((80,))],
        input_output_aliases=aliases,
        compiler_params=params(),
        cost_estimate=cost(0, 2**22),
        name="assemble",
    )(*blocks)


def shards(local, base, momentum):
    z_a, z_b = Z_ORDER[:5], Z_ORDER[5:]
    local = pltpu.with_memory_space_constraint(local, pltpu.HBM)
    base = pltpu.with_memory_space_constraint(base, pltpu.HBM)

    far = tuple((2, dz) for dz in Z_ORDER)
    far_low, far_high = contribute(((0, ROWS_A, far, (4, 4), None),), local, base)
    low, high = shift(far_low, 1, 0), shift(far_high, -1, 0)
    sent_b = tuple((dx, dz) for dz in z_a for dx in range(NX))
    plus_b, minus_b = contribute(
        ((ROWS_A, ROWS_B, sent_b, (10, 10), None),), local, base, far_low
    )
    from_minus_b, from_plus_b = shift(plus_b, 0, 1), shift(minus_b, 0, -1)
    near_x = tuple((dx, dz) for dx in (1, -1) for dz in Z_ORDER)
    near_p, near_m = contribute(((0, ROWS_A, near_x, (8, 8), None),), local, base)

    wide = (ROWS_A, 2048)
    to_p, to_m = call(relay_x_kernel, [(wide, BF)] * 2, near_p, near_m, low, high, name="relay_x")
    r_p, r_m = shift(to_p, 1, 0), shift(to_m, -1, 0)
    own_x = tuple((0, dz) for dz in Z_ORDER)
    kept_b = tuple((dx, dz) for dz in z_b for dx in range(NX))
    own_x, base_a, keep0_b, keep3p_b, keep3m_b, base_b = contribute(
        ((0, ROWS_A, own_x, (8,), 5), (ROWS_A, ROWS_B, kept_b, (4, 4, 4), 0)), local, base
    )

    half = (ROWS_B, NX * W)
    to3p_b, to3m_b = call(
        functools.partial(relay_kernel, NX * W), [(half, BF), (half, BF)],
        keep3p_b, keep3m_b, from_minus_b, from_plus_b, name="relay_b",
    )
    r3p_b, r3m_b = shift(to3p_b, 0, 3), shift(to3m_b, 0, -3)

    strip, group = (ROWS_A, W), (ROWS_A, 640)
    plus_a, minus_a, keep0, keep3p, keep3m = call(
        sum_x_kernel, [(group, BF), (group, BF)] + [(strip, F32)] * 3, own_x, r_p, r_m,
        name="sum_a",
    )
    from_minus, from_plus = shift(plus_a, 0, 1), shift(minus_a, 0, -1)
    to3p, to3m = call(
        functools.partial(relay_kernel, W), [(strip, BF), (strip, BF)],
        keep3p, keep3m, from_minus, from_plus, name="relay_a",
    )
    r3p, r3m = shift(to3p, 0, 3), shift(to3m, 0, -3)

    strip = (ROWS_B, W)
    own, s1, s2, s3 = call(
        sum_z_kernel, [(strip, F32), (strip, BF), (strip, BF), (strip, BF)],
        keep0_b, from_minus_b, from_plus_b, r3p_b, r3m_b, after=(plus_a,), name="sum_b",
    )
    b1, b2, b3 = shift(s1, 1, 0), shift(s2, 2, 0), shift(s3, 3, 0)

    momentum_a, own_a = update(
        update_a_kernel, base_a, momentum[:ROWS_A], keep0, from_minus, from_plus, r3p, r3m
    )
    p3, m3 = shift(own_a, 0, -3), shift(own_a, 0, 3)
    momentum_b, own_b = update(
        update_b_kernel, base_b, momentum[ROWS_A:], own, b1, b2, b3
    )
    b1, b2, b3 = [shift(own_b, e, 0) for e in (1, 2, 3)]
    plus_a, minus_a = join(
        (((0, 0, W), (1, 0, W), (2, 0, 128)), ((0, 0, W), (2, 0, W), (1, 128, 128))),
        own_a, p3, m3, after=(own_b,), name="join_a",
    )
    from_minus, from_plus = shift(plus_a, 0, 1), shift(minus_a, 0, -1)
    (row_b,) = join(
        (((0, 0, W), (1, 0, W), (2, 0, W), (3, 0, W)),),
        own_b, b1, b2, b3, after=(plus_a,), name="join_b",
    )
    p3_b, m3_b = shift(row_b, 0, -3), shift(row_b, 0, 3)
    (row_a,) = join(
        (((0, 0, W), (1, 0, W), (2, 0, W), (3, 0, 640), (4, 0, 640)),),
        own_a, p3, m3, from_minus, from_plus, after=(row_b,), name="join_row_a",
    )
    m1, p1 = shift(row_a, 1, 0), shift(row_a, -1, 0)
    plus_b, minus_b = join(
        (((0, 0, 1024), (1, 0, 1024), (2, 0, 512)), ((0, 0, 1024), (2, 0, 1024), (1, 512, 512))),
        row_b, p3_b, m3_b, name="join_row_b",
    )
    from_minus_b, from_plus_b = shift(plus_b, 0, 1), shift(minus_b, 0, -1)
    low, high = join(
        (((0, 0, 1024),), ((1, 1024, 1024),)), m1, p1, name="relay_row_a"
    )
    low, high = shift(low, 1, 0), shift(high, -1, 0)
    new_momentum = jnp.concatenate([momentum_a, momentum_b], axis=0)
    early = ((0, 0, WHOLE), (0, -1, WHOLE), (0, 1, WHOLE), (1, 0, ONE), (1, 3, ONE), (1, -3, ONE))
    late = ((0, 2, LOW), (0, 2, HIGH), (1, 0, FROM_MINUS), (1, 0, FROM_PLUS))
    partial = assemble(early, row_a, m1, p1, row_b, p3_b, m3_b)
    new_fragment = assemble(late, low, high, from_minus_b, from_plus_b, partial)
    return (new_fragment, new_momentum)


def solution(mesh):
    in_specs = (P("replica", "shard", None), P("shard", None), P("shard", "replica"))
    out_specs = (P("shard", None), P("shard", "replica"))
    return jax.shard_map(shards, mesh=mesh, in_specs=in_specs, out_specs=out_specs, check_vma=False)
```
